32 devices in a mesh: grp: 2 (over y), seq: 4 (over z), req: 2 (over x), hd: 2 (over core).
Axes of the slice: x: 2, y: 2, z: 4, core: 2. Of those that a mesh axis runs over, the one named last changes fastest.
Arguments:
- cache: bfloat16 [8, 8, 1536, 256], P(('grp', 'req'), 'hd', 'seq'), parts along dimension 0, may hold values from -7 to 7
- evicted: bfloat16 [8, 8, 256, 256], P(('grp', 'req'), 'hd', 'seq'), parts along dimension 0, may hold values from -6 to 6
- merge_weight: bfloat16 [8, 8, 256], P(('grp', 'req'), 'hd', 'seq'), parts along dimension 0, may hold values from 0.25 to 2.5
- targets: int32 [8, 8, 256], P(('grp', 'req'), 'hd', 'seq'), parts along dimension 0, may hold values from 0 to 1535, as said below
- kept_counts: int32 [8, 4], P(('grp', 'req'), 'seq'), parts along dimension 0, may hold values from 192 to 384, as said below
- queries: bfloat16 [4, 8, 64, 128], P(None, ('grp', 'req'), 'hd'), parts along dimension 1, may hold values from -1024 to 1024
- new_rows: bfloat16 [4, 8, 8, 256], P(None, ('grp', 'req'), 'hd'), parts along dimension 1, may hold values from -8 to 8
Outputs:
- merged_cache: bfloat16 [8, 8, 1536, 256], P(('grp', 'req'), 'hd', 'seq'), parts along dimension 0
- attended: bfloat16 [4, 8, 64, 128], P(None, ('grp', 'req'), 'hd'), parts along dimension 1
The draws below stay inside these ranges and needn't reach their ends.
There are 2 independent parts, one for each index of `grp`. The reference program is written for one: setup_inputs(seed, part) draws one part's arguments, and reference() takes and returns one part's arrays. A program takes and returns all parts, laid end to end along the dimension named above; each array names one. Nothing has to cross between parts.
Inputs may be any that keep to these rules, and one draw needn't show every extreme that they name: `targets`: for each request, head and block of 64 evicted rows, at most 32 rows target one block of 384 kept positions; every target is a live position. `kept_counts`: each request has a block with all 384 positions live.
All inputs are finite; a program needn't handle non-finite values.
Results may differ from the reference program's by a relative error of at most 0.0029.
Values may be sent and summed in bfloat16 or wider, within the bound.
No kernel may reach another device: no remote copies, remote signals or barrier semaphores. Data moves between devices by JAX's collectives and lax.ppermute only.
A program may use at most 64 MiB of HBM per device.

```python
import math
import jax
import jax.numpy as jnp
from jax import lax

KVH = 8
QH = 64
HEAD = 128
KEPT_DEV = 384
EVICT_DEV = 64
STEPS = 4
REQS = 4
KEPT = 1536
EVICT = 256


def routing_tables(key):
    shards = KEPT // KEPT_DEV
    counts = jax.random.randint(jax.random.fold_in(key, 11), (REQS, shards), KEPT_DEV // 2, KEPT_DEV + 1)
    full_at = jax.random.randint(jax.random.fold_in(key, 12), (REQS,), 0, shards)
    counts = jnp.where(jnp.arange(shards)[None, :] == full_at[:, None], KEPT_DEV, counts)
    capacity = max(2, 2 * EVICT_DEV // shards)
    hottest = jax.random.randint(jax.random.fold_in(key, 13), (REQS, KVH), 0, shards)
    others_total = (shards - 1) * capacity
    spare = EVICT_DEV - capacity
    noise = jax.random.randint(jax.random.fold_in(key, 14), (REQS, KVH, shards, others_total), 0, 1 << 16)
    noise = noise * 4096 + jnp.arange(others_total)
    chosen = jnp.argsort(noise, axis=-1, stable=True)[..., :spare]
    other_dest = chosen // capacity
    other_dest = other_dest + (other_dest >= hottest[:, :, None, None]).astype(jnp.int32)
    hot_dest = jnp.broadcast_to(hottest[:, :, None, None], (REQS, KVH, shards, capacity))
    destination = jnp.concatenate([hot_dest, other_dest], axis=-1)
    shuffle = jax.random.randint(jax.random.fold_in(key, 15), (REQS, KVH, shards, EVICT_DEV), 0, 1 << 16)
    shuffle = shuffle * 4096 + jnp.arange(EVICT_DEV)
    ordering = jnp.argsort(shuffle, axis=-1, stable=True)
    destination = jnp.take_along_axis(destination, ordering, axis=-1)
    count_table = jnp.broadcast_to(counts[:, None, None, :], (REQS, KVH, shards, shards))
    limit = jnp.take_along_axis(count_table, destination, axis=-1)
    position = jax.random.randint(jax.random.fold_in(key, 16), destination.shape, 0, limit)
    aimed = destination * KEPT_DEV + position
    return (counts.astype(jnp.int32), aimed.reshape(REQS, KVH, shards * EVICT_DEV).astype(jnp.int32))


def draw_targets(key, part):
    return routing_tables(key)[1]


def draw_kept_counts(key, part):
    return routing_tables(key)[0]


def draw_cache(key, part):
    shards = KEPT // KEPT_DEV
    key_part = jnp.clip(jax.random.normal(jax.random.fold_in(key, 31), (REQS, KVH, KEPT, HEAD)), -5.0, 5.0)
    offsets = jax.random.uniform(jax.random.fold_in(key, 32), (REQS, KVH, shards, 1, HEAD), minval=-1.5, maxval=1.5)
    value_base = jnp.clip(jax.random.normal(jax.random.fold_in(key, 33), (REQS, KVH, shards, KEPT_DEV, HEAD)), -4.0, 4.0)
    value_part = (value_base + offsets).reshape(REQS, KVH, KEPT, HEAD)
    return jnp.concatenate([key_part, value_part], axis=-1).astype(jnp.bfloat16)


def decode_inputs(key):
    query_key = jax.random.fold_in(key, 21)
    fresh_key = jax.random.fold_in(key, 22)
    asked = jnp.clip(jax.random.normal(query_key, (STEPS, REQS, QH, HEAD)), -6.0, 6.0)
    fresh = jnp.clip(jax.random.normal(fresh_key, (STEPS, REQS, KVH, 2 * HEAD)), -6.0, 6.0)
    return (asked, fresh)


def draw_queries(key, part):
    return decode_inputs(key)[0].astype(jnp.bfloat16)


def draw_new_rows(key, part):
    return decode_inputs(key)[1].astype(jnp.bfloat16)


def shard_levels(rng, extent, pieces, smallest, largest):
    def one(dim, parts):
        heights = jax.random.uniform(jax.random.fold_in(jax.random.fold_in(rng, 6), dim), (parts,), jnp.float32, smallest / len(pieces), largest / len(pieces))
        return jnp.repeat(jnp.exp(heights), extent[dim] // parts).reshape((-1,) + (1,) * (len(extent) - dim - 1))

    gain = one(*pieces[0])
    for cut in pieces[1:]:
        gain = gain * one(*cut)
    return gain


def centred(rng, dims, spread, bound, pieces=(), kind=jnp.bfloat16):
    array = jax.random.normal(rng, dims, jnp.float32) * spread
    if len(pieces) > 0:
        array = shard_levels(rng, dims, pieces, -0.22, 0.18) * array
    return jnp.clip(array, min=-bound, max=bound).astype(kind)


def setup_inputs(seed: int = 0, part: int = 0) -> dict:
    splits = jax.random.split(jax.random.key(seed), 8)
    own_keys = jax.random.split(jax.random.fold_in(splits[7], part), 8)
    return {
        "cache": draw_cache(jax.random.fold_in(jax.random.fold_in(splits[7], part), 71), part),
        "evicted": centred(own_keys[1], (REQS, KVH, EVICT, 2 * HEAD), 1.0, 6.0, ((0, 2), (1, 2), (2, 4))),
        "merge_weight": jnp.clip(jnp.exp(math.log(2.5) - 2.3025851 * jax.random.uniform(own_keys[2], (REQS, KVH, EVICT), jnp.float32) ** shard_levels(own_keys[2], (REQS, KVH, EVICT), ((0, 2), (1, 2), (2, 4)), -0.2, 0.2)), 0.25, 2.5).astype(jnp.bfloat16),
        "targets": draw_targets(jax.random.fold_in(jax.random.fold_in(splits[7], part), 71), part),
        "kept_counts": draw_kept_counts(jax.random.fold_in(jax.random.fold_in(splits[7], part), 71), part),
        "queries": draw_queries(jax.random.fold_in(jax.random.fold_in(splits[7], part), 71), part),
        "new_rows": draw_new_rows(jax.random.fold_in(jax.random.fold_in(splits[7], part), 71), part),
    }


def merge_head(inputs):
    stored, removed, weights, target_rows = inputs
    weight_f = weights.astype(jnp.float32)
    summed = jax.ops.segment_sum(weight_f[:, None] * removed.astype(jnp.float32), target_rows, num_segments=KEPT)
    weight_sum = jax.ops.segment_sum(weight_f, target_rows, num_segments=KEPT)
    return ((stored.astype(jnp.float32) + summed) / (1.0 + weight_sum)[:, None]).astype(jnp.bfloat16)

def round_weights(values):
    rounded = values.astype(jnp.bfloat16)
    rounded = lax.optimization_barrier(rounded)
    return rounded.astype(jnp.float32)

def attend_request(inputs):
    stored, counts, asked_rows, fresh_rows = inputs
    group_size = QH // KVH
    blocks_count = KEPT // KEPT_DEV
    scale_factor = 1.0 / math.sqrt(HEAD)
    query_rows = asked_rows.reshape(STEPS, KVH, group_size, HEAD).transpose(1, 0, 2, 3)
    query_rows = query_rows.reshape(KVH, STEPS * group_size, HEAD).astype(jnp.float32)
    key_blocks = stored[:, :, :HEAD].astype(jnp.float32).reshape(KVH, blocks_count, KEPT_DEV, HEAD)
    value_blocks = stored[:, :, HEAD:].astype(jnp.float32).reshape(KVH, blocks_count, KEPT_DEV, HEAD)
    scores = jnp.einsum('hqd,hbkd->hbqk', query_rows, key_blocks) * scale_factor
    living = jnp.arange(KEPT_DEV, dtype=jnp.int32)[None, :] < counts[:, None]
    scores = jnp.where(living[None, :, None, :], scores, -1e+30)
    block_max = lax.optimization_barrier(jnp.max(scores, axis=-1))
    exponent = jnp.exp(scores - block_max[..., None])
    block_sum = lax.optimization_barrier(jnp.sum(exponent, axis=-1))
    block_acc = jnp.einsum('hbqk,hbkd->hbqd', round_weights(exponent), value_blocks)
    fresh_heads = fresh_rows.transpose(1, 0, 2).astype(jnp.float32)
    new_scores = jnp.einsum('hqd,hjd->hqj', query_rows, fresh_heads[:, :, :HEAD]) * scale_factor
    step_index = jnp.arange(STEPS * group_size, dtype=jnp.int32) // group_size
    allowed = jnp.arange(STEPS, dtype=jnp.int32)[None, :] <= step_index[:, None]
    new_scores = jnp.where(allowed[None], new_scores, -1e+30)
    new_max = lax.optimization_barrier(jnp.max(new_scores, axis=-1))
    new_exponent = jnp.exp(new_scores - new_max[..., None])
    new_sum = lax.optimization_barrier(jnp.sum(new_exponent, axis=-1))
    new_acc = jnp.einsum('hqj,hjd->hqd', round_weights(new_exponent), fresh_heads[:, :, HEAD:])
    highest = jnp.maximum(lax.optimization_barrier(jnp.max(block_max, axis=1)), new_max)
    block_scale = jnp.exp(block_max - highest[:, None, :])
    new_scale = jnp.exp(new_max - highest)
    denominator = lax.optimization_barrier(jnp.sum(block_sum * block_scale, axis=1)) + new_sum * new_scale
    numerator = lax.optimization_barrier(jnp.sum(block_acc * block_scale[..., None], axis=1)) + new_acc * new_scale[..., None]
    result = (numerator / denominator[..., None]).astype(jnp.bfloat16)
    result = result.reshape(KVH, STEPS, group_size, HEAD).transpose(1, 0, 2, 3)
    return result.reshape(STEPS, QH, HEAD)

def reference(cache, evicted, merge_weight, targets, kept_counts, queries, new_rows):
    merged_flat = lax.map(merge_head, (cache.reshape(REQS * KVH, KEPT, 2 * HEAD), evicted.reshape(REQS * KVH, EVICT, 2 * HEAD), merge_weight.reshape(REQS * KVH, EVICT), targets.reshape(REQS * KVH, EVICT)))
    merged_cache = merged_flat.reshape(REQS, KVH, KEPT, 2 * HEAD)
    attended = lax.map(attend_request, (merged_cache, kept_counts, queries.transpose(1, 0, 2, 3), new_rows.transpose(1, 0, 2, 3)))
    return (merged_cache, attended.transpose(1, 0, 2, 3))
```

```python
import functools
import math

import jax
import jax.numpy as jnp
from jax import lax
from jax.experimental import pallas as pl
from jax.experimental.pallas import tpu as pltpu
from jax.sharding import PartitionSpec as P

META_ROWS = 16
STAT_ROWS = 8
VMEM_BYTES = 32 * 1024 * 1024


def dot(a, b, contract):
    return lax.dot_general(a, b, (contract, ((), ())), preferred_element_type=jnp.float32)


def pack_kernel(shards, capacity, kept_dev, evicted_ref, weight_ref, target_ref, *message_refs):
    pairs, evict_dev, width = evicted_ref.shape
    slots = shards * capacity
    me = lax.axis_index("seq")
    targets = target_ref[...]
    holder = jnp.zeros_like(targets)
    for block in range(1, shards):
        holder += (targets >= block * kept_dev).astype(jnp.int32)
    centred = targets - holder * kept_dev - kept_dev // 2
    distance = jnp.where(holder >= me, holder - me, holder - me + shards)
    owned = jnp.concatenate(
        [(distance == k).astype(jnp.float32) for k in range(shards)], axis=0
    )
    before = lax.broadcasted_iota(jnp.int32, (evict_dev, evict_dev), 0) < lax.broadcasted_iota(
        jnp.int32, (evict_dev, evict_dev), 1
    )
    prefix = dot(owned.astype(jnp.bfloat16), before.astype(jnp.bfloat16), ((1,), (0,)))
    ranked = owned * prefix
    rank = ranked[0:pairs]
    for k in range(1, shards):
        rank += ranked[k * pairs : (k + 1) * pairs]
    slot = distance * capacity + rank.astype(jnp.int32)
    facts = jnp.concatenate(
        [weight_ref[...].astype(jnp.float32), centred.astype(jnp.float32)], axis=0
    ).astype(jnp.bfloat16)
    slot_index = lax.broadcasted_iota(jnp.int32, (slots, evict_dev), 0)
    pair_index = lax.broadcasted_iota(jnp.int32, (pairs, slots), 0)
    weights = jnp.zeros((pairs, slots), jnp.float32)
    positions = jnp.zeros((pairs, slots), jnp.float32)
    rows = []
    for p in range(pairs):
        placing = (slot_index == slot[p : p + 1, :]).astype(jnp.float32).astype(jnp.bfloat16)
        rows.append(dot(placing, evicted_ref[p], ((1,), (0,))))
        placed = dot(facts, placing, ((1,), (1,)))
        weights = jnp.where(pair_index == p, placed[0:pairs], weights)
        positions = jnp.where(pair_index == p, placed[pairs : 2 * pairs], positions)
    meta = jnp.concatenate([weights, positions], axis=1)
    meta = jnp.concatenate([meta, jnp.zeros((META_ROWS - pairs, 2 * slots), jnp.float32)], axis=0)
    meta = meta.astype(jnp.bfloat16)
    for k in range(shards):
        message = [r[k * capacity : (k + 1) * capacity] for r in rows]
        message_refs[k][0 : pairs * capacity, :] = jnp.concatenate(message, axis=0).astype(
            jnp.bfloat16
        )
        message_refs[k][pairs * capacity : pairs * capacity + META_ROWS, :] = meta


def merge_kernel(shards, capacity, heads, *refs):
    cache_ref, query_ref, count_ref = refs[:3]
    message_refs = refs[3 : 3 + shards]
    merged_ref, partial_ref, cache_buf, merged_buf, in_sem, out_sem = refs[3 + shards :]
    pairs, kept_dev, width = cache_buf.shape
    head_dim = width // 2
    rows_each = query_ref.shape[1]
    slots = shards * capacity
    scale = 1.0 / math.sqrt(head_dim)
    loads = [
        pltpu.make_async_copy(cache_ref.at[p], cache_buf.at[p], in_sem.at[p]) for p in range(pairs)
    ]
    stores = [
        pltpu.make_async_copy(merged_buf.at[p], merged_ref.at[p], out_sem.at[p])
        for p in range(pairs)
    ]
    for load in loads:
        load.start()
    lane = lax.broadcasted_iota(jnp.int32, (pairs, slots), 1)
    weights = jnp.zeros((pairs, slots), jnp.float32)
    positions = jnp.zeros((pairs, slots), jnp.float32)
    received = []
    for k in range(shards):
        meta = message_refs[k][pairs * capacity : pairs * capacity + META_ROWS, :]
        meta = meta.astype(jnp.float32)[0:pairs]
        mine = jnp.logical_and(lane >= k * capacity, lane < (k + 1) * capacity)
        weights = jnp.where(mine, meta[:, 0:slots], weights)
        positions = jnp.where(mine, meta[:, slots : 2 * slots], positions)
        if capacity % 16:
            received.append(message_refs[k][0 : pairs * capacity, :].astype(jnp.float32))
    positions = (positions + float(kept_dev // 2)).astype(jnp.int32)
    kept_index = lax.broadcasted_iota(jnp.int32, (kept_dev, slots), 0)
    column = lax.broadcasted_iota(jnp.int32, (rows_each, kept_dev), 1)
    ones = jnp.ones((slots, head_dim), jnp.bfloat16)
    tops, totals = [], []
    for p in range(pairs):
        if capacity % 16:
            rows = [r[p * capacity : (p + 1) * capacity] for r in received]
            rows = jnp.concatenate(rows, axis=0).astype(jnp.bfloat16)
        else:
            rows = [m[p * capacity : (p + 1) * capacity, :] for m in message_refs]
            rows = jnp.concatenate(rows, axis=0)
        placing = jnp.where(kept_index == positions[p : p + 1, :], weights[p : p + 1, :], 0.0)
        placing = placing.astype(jnp.bfloat16)
        summed = dot(placing, rows, ((1,), (0,)))
        share = 1.0 / (1.0 + dot(placing, ones, ((1,), (0,))))
        loads[p].wait()
        stored = cache_buf[p].astype(jnp.float32) + summed
        keys = (stored[:, 0:head_dim] * share).astype(jnp.bfloat16)
        values = (stored[:, head_dim:] * share).astype(jnp.bfloat16)
        merged_buf[p, :, 0:head_dim] = keys
        merged_buf[p, :, head_dim:] = values
        stores[p].start()
        scores = dot(query_ref[p], keys, ((1,), (1,))) * scale
        scores = jnp.where(column < count_ref[p // heads, 0], scores, -1e30)
        top = jnp.max(scores, axis=1, keepdims=True)
        exponent = jnp.exp(scores - top)
        tops.append(top)
        totals.append(jnp.sum(exponent, axis=1, keepdims=True))
        partial_ref[p * rows_each : (p + 1) * rows_each, :] = dot(
            exponent.astype(jnp.bfloat16), values, ((1,), (0,))
        )
    stat_lane = lax.broadcasted_iota(jnp.int32, (heads * rows_each, head_dim), 1)
    stats = []
    for first in range(0, pairs, heads):
        top = jnp.concatenate(tops[first : first + heads], axis=0)
        total = jnp.concatenate(totals[first : first + heads], axis=0)
        both = jnp.where(stat_lane == 0, top, jnp.where(stat_lane == 1, total, 0.0))
        stats.append(jnp.transpose(both)[0:2, :])
    stats.append(jnp.zeros((STAT_ROWS - 2 * (pairs // heads), head_dim), jnp.float32))
    partial_ref[pairs * rows_each : pairs * rows_each + STAT_ROWS, :] = jnp.concatenate(
        stats, axis=0
    )
    for store in stores:
        store.wait()


def combine_kernel(shards, heads, *refs):
    partial_refs = refs[:shards]
    fresh_top_ref, fresh_total_ref, fresh_ref, out_ref, ordered = refs[shards:]
    steps, requests, query_local, head_dim = out_ref.shape
    group = query_local // heads
    rows_each = steps * group
    rows_request = heads * rows_each
    me = lax.axis_index("seq")
    for k in range(shards):
        source = jnp.where(me >= k, me - k, me - k + shards)
        ordered[source] = partial_refs[k][...]
    for r in range(requests):
        tops, totals = [fresh_top_ref[r : r + 1, :]], [fresh_total_ref[r : r + 1, :]]
        for b in range(shards):
            first = requests * rows_request + 2 * r
            tops.append(ordered[b, first : first + 1, :])
            totals.append(ordered[b, first + 1 : first + 2, :])
        highest = functools.reduce(jnp.maximum, tops)
        scales = [jnp.exp(top - highest) for top in tops]
        total = sum(a * b for a, b in zip(totals, scales))
        factors = jnp.concatenate([s / total for s in scales], axis=0)
        padding = -(shards + 1) % 8
        if padding:
            factors = jnp.concatenate(
                [factors, jnp.zeros((padding, rows_request), jnp.float32)], axis=0
            )
        factors = jnp.transpose(factors)
        first = r * rows_request
        result = fresh_ref[first : first + rows_request, :] * factors[:, 0:1]
        for b in range(shards):
            result += ordered[b, first : first + rows_request, :] * factors[:, b + 1 : b + 2]
        for s in range(steps):
            pieces = [
                result[h * rows_each + s * group : h * rows_each + (s + 1) * group]
                for h in range(heads)
            ]
            out_ref[s, r] = jnp.concatenate(pieces, axis=0).astype(jnp.bfloat16)


def fresh_block(query_rows, fresh_rows, group):
    head_dim = query_rows.shape[-1]
    scores = jnp.einsum(
        "pqd,pjd->pqj", query_rows, fresh_rows[..., :head_dim], preferred_element_type=jnp.float32
    ) * (1.0 / math.sqrt(head_dim))
    step_index = jnp.arange(query_rows.shape[1], dtype=jnp.int32) // group
    allowed = jnp.arange(fresh_rows.shape[1], dtype=jnp.int32)[None, :] <= step_index[:, None]
    scores = jnp.where(allowed[None], scores, -1e30)
    top = jnp.max(scores, axis=-1)
    exponent = jnp.exp(scores - top[..., None])
    weighted = jnp.einsum(
        "pqj,pjd->pqd",
        exponent.astype(jnp.bfloat16),
        fresh_rows[..., head_dim:],
        preferred_element_type=jnp.float32,
    )
    return (top, jnp.sum(exponent, axis=-1), weighted)


def body(cache, evicted, merge_weight, targets, kept_counts, queries, new_rows):
    req_local, head_local, kept_dev, width = cache.shape
    head_dim = width // 2
    shards = lax.axis_size("seq")
    evict_dev = evicted.shape[2]
    capacity = max(2, 2 * evict_dev // shards)
    pairs = req_local * head_local
    steps, _, query_local, _ = queries.shape
    group = query_local // head_local
    rows_each = steps * group
    vmem = pl.BlockSpec(memory_space=pltpu.VMEM)
    smem = pl.BlockSpec(memory_space=pltpu.SMEM)
    anywhere = pl.BlockSpec(memory_space=pl.ANY)
    params = pltpu.CompilerParams(vmem_limit_bytes=VMEM_BYTES)

    message = jax.ShapeDtypeStruct((pairs * capacity + META_ROWS, width), jnp.bfloat16)
    messages = pl.pallas_call(
        functools.partial(pack_kernel, shards, capacity, kept_dev),
        out_shape=[message] * shards,
        in_specs=[vmem] * 3,
        out_specs=[vmem] * shards,
        compiler_params=params,
        name="pack",
    )(
        evicted.reshape(pairs, evict_dev, width),
        merge_weight.reshape(pairs, evict_dev),
        targets.reshape(pairs, evict_dev),
    )

    def shifted(array, k):
        return lax.ppermute(array, "seq", [(i, (i + k) % shards) for i in range(shards)])

    messages = [messages[0]] + [shifted(messages[k], k) for k in range(1, shards)]

    query_rows = queries.reshape(steps, req_local, head_local, group, head_dim)
    query_rows = query_rows.transpose(1, 2, 0, 3, 4).reshape(pairs, rows_each, head_dim)
    fresh_rows = new_rows.transpose(1, 2, 0, 3).reshape(pairs, steps, width)
    fresh_top, fresh_total, fresh = fresh_block(query_rows, fresh_rows, group)

    merged, partial = pl.pallas_call(
        functools.partial(merge_kernel, shards, capacity, head_local),
        out_shape=[
            jax.ShapeDtypeStruct((pairs, kept_dev, width), jnp.bfloat16),
            jax.ShapeDtypeStruct((pairs * rows_each + STAT_ROWS, head_dim), jnp.float32),
        ],
        in_specs=[anywhere, vmem, smem] + [vmem] * shards,
        out_specs=[anywhere, vmem],
        scratch_shapes=[
            pltpu.VMEM((pairs, kept_dev, width), jnp.bfloat16),
            pltpu.VMEM((pairs, kept_dev, width), jnp.bfloat16),
            pltpu.SemaphoreType.DMA((pairs,)),
            pltpu.SemaphoreType.DMA((pairs,)),
        ],
        compiler_params=params,
        name="merge",
    )(cache.reshape(pairs, kept_dev, width), query_rows, kept_counts, *messages)

    partials = [partial] + [shifted(partial, k) for k in range(shards - 1, 0, -1)][::-1]

    attended = pl.pallas_call(
        functools.partial(combine_kernel, shards, head_local),
        out_shape=jax.ShapeDtypeStruct(queries.shape, jnp.bfloat16),
        in_specs=[vmem] * (shards + 3),
        out_specs=vmem,
        scratch_shapes=[pltpu.VMEM((shards,) + partial.shape, jnp.float32)],
        compiler_params=params,
        name="combine",
    )(
        *partials,
        fresh_top.reshape(req_local, head_local * rows_each),
        fresh_total.reshape(req_local, head_local * rows_each),
        fresh.reshape(pairs * rows_each, head_dim),
    )
    return (merged.reshape(cache.shape), attended)


def solution(mesh):
    return jax.shard_map(
        body,
        mesh=mesh,
        in_specs=(
            P(("grp", "req"), "hd", "seq", None),
            P(("grp", "req"), "hd", "seq", None),
            P(("grp", "req"), "hd", "seq"),
            P(("grp", "req"), "hd", "seq"),
            P(("grp", "req"), "seq"),
            P(None, ("grp", "req"), "hd", None),
            P(None, ("grp", "req"), "hd", None),
        ),
        out_specs=(P(("grp", "req"), "hd", "seq", None), P(None, ("grp", "req"), "hd", None)),
        check_vma=False,
    )
```

```python
import functools
import math

import jax
import jax.numpy as jnp
from jax import lax
from jax.experimental import pallas as pl
from jax.experimental.pallas import tpu as pltpu
from jax.sharding import PartitionSpec as P

META_ROWS = 16
STATS = 4
CODE_MAX = 32767.0
LEVELS = 16.0
SMALLEST = 1e-36
FRACTION = 2.0**30
VMEM_BYTES = 8 * 1024 * 1024


def dot(a, b, contract):
    return lax.dot_general(a, b, (contract, ((), ())), preferred_element_type=jnp.float32)


def pack_kernel(shards, capacity, kept_dev, *refs):
    message_refs = refs[3 : 3 + shards]
    evicted_ref, weight_ref, target_ref, sems = refs[3 + shards :]
    loads = [
        pltpu.make_async_copy(refs[i], refs[3 + shards + i], sems.at[i]) for i in (2, 1, 0)
    ]
    for load in loads:
        load.start()
    pairs, evict_dev, width = evicted_ref.shape
    slots = shards * capacity
    me = lax.axis_index("seq")
    loads[0].wait()
    loads[1].wait()
    targets = target_ref[...]
    holder = jnp.zeros_like(targets)
    for block in range(1, shards):
        holder += (targets >= block * kept_dev).astype(jnp.int32)
    centred = targets - holder * kept_dev - kept_dev // 2
    distance = jnp.where(holder >= me, holder - me, holder - me + shards)
    owned = jnp.concatenate(
        [(distance == k).astype(jnp.float32) for k in range(shards)], axis=0
    )
    before = lax.broadcasted_iota(jnp.int32, (evict_dev, evict_dev), 0) < lax.broadcasted_iota(
        jnp.int32, (evict_dev, evict_dev), 1
    )
    prefix = dot(owned.astype(jnp.bfloat16), before.astype(jnp.bfloat16), ((1,), (0,)))
    ranked = owned * prefix
    rank = ranked[0:pairs]
    for k in range(1, shards):
        rank += ranked[k * pairs : (k + 1) * pairs]
    slot = distance * capacity + rank.astype(jnp.int32)
    facts = jnp.concatenate(
        [weight_ref[...].astype(jnp.float32), centred.astype(jnp.float32)], axis=0
    ).astype(jnp.bfloat16)
    slot_index = lax.broadcasted_iota(jnp.int32, (slots, evict_dev), 0)
    pair_index = lax.broadcasted_iota(jnp.int32, (pairs, slots), 0)
    weights = jnp.zeros((pairs, slots), jnp.float32)
    positions = jnp.zeros((pairs, slots), jnp.float32)
    rows = []
    loads[2].wait()
    for p in range(pairs):
        placing = (slot_index == slot[p : p + 1, :]).astype(jnp.float32).astype(jnp.bfloat16)
        rows.append(dot(placing, evicted_ref[p], ((1,), (0,))))
        placed = dot(facts, placing, ((1,), (1,)))
        weights = jnp.where(pair_index == p, placed[0:pairs], weights)
        positions = jnp.where(pair_index == p, placed[pairs : 2 * pairs], positions)
    meta = jnp.concatenate([weights, positions], axis=1)
    meta = jnp.concatenate([meta, jnp.zeros((META_ROWS - pairs, 2 * slots), jnp.float32)], axis=0)
    meta = meta.astype(jnp.bfloat16)
    for k in range(shards):
        message = [r[k * capacity : (k + 1) * capacity] for r in rows]
        message_refs[k][0 : pairs * capacity, :] = jnp.concatenate(message, axis=0).astype(
            jnp.bfloat16
        )
        message_refs[k][pairs * capacity : pairs * capacity + META_ROWS, :] = meta


def copy_kernel(from_ref, to_ref, sem):
    copy = pltpu.make_async_copy(from_ref, to_ref, sem)
    copy.start()
    copy.wait()


def merge_kernel(shards, capacity, heads, *refs):
    cache_ref, query_ref, count_ref = refs[:3]
    message_refs = refs[3 : 3 + shards]
    merged_ref, partial_ref = refs[3 + shards :]
    pairs, kept_dev, width = merged_ref.shape
    head_dim = width // 2
    rows_each = query_ref.shape[1]
    slots = shards * capacity
    scale = 1.0 / math.sqrt(head_dim)
    lane = lax.broadcasted_iota(jnp.int32, (pairs, slots), 1)
    weights = jnp.zeros((pairs, slots), jnp.float32)
    positions = jnp.zeros((pairs, slots), jnp.float32)
    received = []
    for k in range(shards):
        meta = message_refs[k][pairs * capacity : pairs * capacity + META_ROWS, :]
        meta = meta.astype(jnp.float32)[0:pairs]
        mine = jnp.logical_and(lane >= k * capacity, lane < (k + 1) * capacity)
        weights = jnp.where(mine, meta[:, 0:slots], weights)
        positions = jnp.where(mine, meta[:, slots : 2 * slots], positions)
        if capacity % 16:
            received.append(message_refs[k][0 : pairs * capacity, :].astype(jnp.float32))
    positions = (positions + float(kept_dev // 2)).astype(jnp.int32)
    kept_index = lax.broadcasted_iota(jnp.int32, (kept_dev, slots), 0)
    ones = jnp.ones((slots, head_dim), jnp.bfloat16)
    for p in range(pairs):
        if capacity % 16:
            rows = [r[p * capacity : (p + 1) * capacity] for r in received]
            rows = jnp.concatenate(rows, axis=0).astype(jnp.bfloat16)
        else:
            rows = [m[p * capacity : (p + 1) * capacity, :] for m in message_refs]
            rows = jnp.concatenate(rows, axis=0)
        placing = jnp.where(kept_index == positions[p : p + 1, :], weights[p : p + 1, :], 0.0)
        placing = placing.astype(jnp.bfloat16)
        summed = dot(placing, rows, ((1,), (0,)))
        share = 1.0 / (1.0 + dot(placing, ones, ((1,), (0,))))
        stored = cache_ref[p].astype(jnp.float32) + summed
        merged_ref[p, :, 0:head_dim] = (stored[:, 0:head_dim] * share).astype(jnp.bfloat16)
        merged_ref[p, :, head_dim:] = (stored[:, head_dim:] * share).astype(jnp.bfloat16)
    column = lax.broadcasted_iota(jnp.int32, (heads * rows_each, kept_dev), 1)
    stat_lane = lax.broadcasted_iota(jnp.int32, (heads * rows_each, head_dim), 1)
    codes, stats = [], []
    for r in range(pairs // heads):
        own = range(r * heads, (r + 1) * heads)
        scores = [dot(query_ref[p], merged_ref[p, :, 0:head_dim], ((1,), (1,))) for p in own]
        scores = jnp.concatenate(scores, axis=0) * scale
        scores = jnp.where(column < count_ref[r, 0], scores, -1e30)
        top = jnp.max(scores, axis=1, keepdims=True)
        exponent = jnp.exp(scores - top)
        total = jnp.sum(exponent, axis=1, keepdims=True)
        exponent = exponent.astype(jnp.bfloat16)
        weighted = [
            dot(
                exponent[i * rows_each : (i + 1) * rows_each],
                merged_ref[p, :, head_dim:],
                ((1,), (0,)),
            )
            for i, p in enumerate(own)
        ]
        weighted = jnp.concatenate(weighted, axis=0)
        largest = jnp.max(jnp.abs(weighted), axis=1, keepdims=True)
        level = jnp.ceil(jnp.log2(jnp.maximum(largest, SMALLEST)) * LEVELS)
        code = jnp.floor(weighted * (CODE_MAX / jnp.exp2(level / LEVELS)) + 0.5)
        codes.append(jnp.clip(code, -CODE_MAX, CODE_MAX).astype(jnp.int32))
        both = jnp.where(stat_lane == 0, top, jnp.where(stat_lane == 1, total, level))
        both = jnp.transpose(both)
        top, total, level = both[0:1], both[1:2], both[2:3]
        whole = jnp.floor(top)
        stats.append(whole.astype(jnp.int32))
        stats.append(((top - whole) * FRACTION).astype(jnp.int32))
        stats.append((total * (FRACTION / kept_dev)).astype(jnp.int32))
        stats.append(level.astype(jnp.int32))
    codes = jnp.concatenate(codes, axis=0)
    half = pairs * rows_each // 2
    partial_ref[0:half, :] = (codes[0:half] << 16) | (codes[half:] & 0xFFFF)
    partial_ref[half:, :] = jnp.concatenate(stats, axis=0)


def combine_kernel(shards, heads, kept_dev, *refs):
    partial_refs = refs[:shards]
    fresh_top_ref, fresh_total_ref, fresh_ref, out_ref, ordered = refs[shards:]
    steps, requests, query_local, head_dim = out_ref.shape
    group = query_local // heads
    rows_each = steps * group
    rows_request = heads * rows_each
    half = requests * rows_request // 2
    me = lax.axis_index("seq")
    for k in range(shards):
        source = jnp.where(me >= k, me - k, me - k + shards)
        ordered[source] = partial_refs[k][...]
    for r in range(requests):
        tops, totals, units = [fresh_top_ref[r : r + 1, :]], [fresh_total_ref[r : r + 1, :]], [1.0]
        for b in range(shards):
            stats = ordered[b, half + r * STATS : half + (r + 1) * STATS, :].astype(jnp.float32)
            tops.append(stats[0:1] + stats[1:2] * (1.0 / FRACTION))
            totals.append(stats[2:3] * (kept_dev / FRACTION))
            units.append(jnp.exp2(stats[3:4] / LEVELS) * (1.0 / CODE_MAX))
        highest = functools.reduce(jnp.maximum, tops)
        scales = [jnp.exp(top - highest) for top in tops]
        total = sum(a * b for a, b in zip(totals, scales))
        factors = jnp.concatenate([s * u / total for s, u in zip(scales, units)], axis=0)
        padding = -(shards + 1) % 8
        if padding:
            factors = jnp.concatenate(
                [factors, jnp.zeros((padding, rows_request), jnp.float32)], axis=0
            )
        factors = jnp.transpose(factors)
        first = r * rows_request
        result = fresh_ref[first : first + rows_request, :] * factors[:, 0:1]
        low = first % half
        for b in range(shards):
            words = ordered[b, low : low + rows_request, :]
            codes = words >> 16 if first < half else (words << 16) >> 16
            result += codes.astype(jnp.float32) * factors[:, b + 1 : b + 2]
        for s in range(steps):
            pieces = [
                result[h * rows_each + s * group : h * rows_each + (s + 1) * group]
                for h in range(heads)
            ]
            out_ref[s, r] = jnp.concatenate(pieces, axis=0).astype(jnp.bfloat16)


def fresh_block(query_rows, fresh_rows, group):
    head_dim = query_rows.shape[-1]
    scores = jnp.einsum(
        "pqd,pjd->pqj", query_rows, fresh_rows[..., :head_dim], preferred_element_type=jnp.float32
    ) * (1.0 / math.sqrt(head_dim))
    step_index = jnp.arange(query_rows.shape[1], dtype=jnp.int32) // group
    allowed = jnp.arange(fresh_rows.shape[1], dtype=jnp.int32)[None, :] <= step_index[:, None]
    scores = jnp.where(allowed[None], scores, -1e30)
    top = jnp.max(scores, axis=-1)
    exponent = jnp.exp(scores - top[..., None])
    weighted = jnp.einsum(
        "pqj,pjd->pqd",
        exponent.astype(jnp.bfloat16),
        fresh_rows[..., head_dim:],
        preferred_element_type=jnp.float32,
    )
    return (top, jnp.sum(exponent, axis=-1), weighted)


def body(cache, evicted, merge_weight, targets, kept_counts, queries, new_rows):
    req_local, head_local, kept_dev, width = cache.shape
    head_dim = width // 2
    shards = lax.axis_size("seq")
    evict_dev = evicted.shape[2]
    capacity = max(2, 2 * evict_dev // shards)
    pairs = req_local * head_local
    steps, _, query_local, _ = queries.shape
    group = query_local // head_local
    rows_each = steps * group
    vmem = pl.BlockSpec(memory_space=pltpu.VMEM)
    smem = pl.BlockSpec(memory_space=pltpu.SMEM)
    anywhere = pl.BlockSpec(memory_space=pl.ANY)

    def in_hbm(array):
        return pltpu.with_memory_space_constraint(array, pltpu.HBM)

    params = pltpu.CompilerParams(vmem_limit_bytes=VMEM_BYTES)

    message = jax.ShapeDtypeStruct((pairs * capacity + META_ROWS, width), jnp.bfloat16)
    messages = pl.pallas_call(
        functools.partial(pack_kernel, shards, capacity, kept_dev),
        out_shape=[message] * shards,
        in_specs=[anywhere] * 3,
        out_specs=[vmem] * shards,
        scratch_shapes=[
            pltpu.VMEM((pairs, evict_dev, width), jnp.bfloat16),
            pltpu.VMEM((pairs, evict_dev), jnp.bfloat16),
            pltpu.VMEM((pairs, evict_dev), jnp.int32),
            pltpu.SemaphoreType.DMA((3,)),
        ],
        compiler_params=params,
        name="pack",
    )(
        in_hbm(evicted.reshape(pairs, evict_dev, width)),
        in_hbm(merge_weight.reshape(pairs, evict_dev)),
        in_hbm(targets.reshape(pairs, evict_dev)),
    )

    def shifted(array, k):
        return lax.ppermute(array, "seq", [(i, (i + k) % shards) for i in range(shards)])

    messages = [messages[0]] + [shifted(messages[k], k) for k in range(1, shards)]

    query_rows = queries.reshape(steps, req_local, head_local, group, head_dim)
    query_rows = query_rows.transpose(1, 2, 0, 3, 4).reshape(pairs, rows_each, head_dim)
    fresh_rows = new_rows.transpose(1, 2, 0, 3).reshape(pairs, steps, width)
    fresh_top, fresh_total, fresh = fresh_block(query_rows, fresh_rows, group)

    staged = pl.pallas_call(
        copy_kernel,
        out_shape=jax.ShapeDtypeStruct((pairs, kept_dev, width), jnp.bfloat16),
        in_specs=[anywhere],
        out_specs=vmem,
        scratch_shapes=[pltpu.SemaphoreType.DMA],
        compiler_params=params,
        name="stage",
    )(in_hbm(cache.reshape(pairs, kept_dev, width)))

    half = pairs * rows_each // 2
    merged, partial = pl.pallas_call(
        functools.partial(merge_kernel, shards, capacity, head_local),
        out_shape=[
            jax.ShapeDtypeStruct((pairs, kept_dev, width), jnp.bfloat16),
            jax.ShapeDtypeStruct((half + STATS * req_local, head_dim), jnp.int32),
        ],
        in_specs=[vmem, vmem, smem] + [vmem] * shards,
        out_specs=[vmem, vmem],
        input_output_aliases={0: 0},
        compiler_params=params,
        name="merge",
    )(staged, query_rows, kept_counts, *messages)

    partials = [partial] + [shifted(partial, k) for k in range(shards - 1, 0, -1)][::-1]

    merged = pl.pallas_call(
        copy_kernel,
        out_shape=pltpu.HBM((pairs, kept_dev, width), jnp.bfloat16),
        in_specs=[vmem],
        out_specs=anywhere,
        scratch_shapes=[pltpu.SemaphoreType.DMA],
        compiler_params=params,
        name="unstage",
    )(merged)

    attended = pl.pallas_call(
        functools.partial(combine_kernel, shards, head_local, kept_dev),
        out_shape=jax.ShapeDtypeStruct(queries.shape, jnp.bfloat16),
        in_specs=[vmem] * (shards + 3),
        out_specs=vmem,
        scratch_shapes=[pltpu.VMEM((shards,) + partial.shape, jnp.int32)],
        compiler_params=params,
        name="combine",
    )(
        *partials,
        fresh_top.reshape(req_local, head_local * rows_each),
        fresh_total.reshape(req_local, head_local * rows_each),
        fresh.reshape(pairs * rows_each, head_dim),
    )
    return (merged.reshape(cache.shape), attended)


def solution(mesh):
    return jax.shard_map(
        body,
        mesh=mesh,
        in_specs=(
            P(("grp", "req"), "hd", "seq", None),
            P(("grp", "req"), "hd", "seq", None),
            P(("grp", "req"), "hd", "seq"),
            P(("grp", "req"), "hd", "seq"),
            P(("grp", "req"), "seq"),
            P(None, ("grp", "req"), "hd", None),
            P(None, ("grp", "req"), "hd", None),
        ),
        out_specs=(P(("grp", "req"), "hd", "seq", None), P(None, ("grp", "req"), "hd", None)),
        check_vma=False,
    )
```

```python
import functools
import math

import jax
import jax.numpy as jnp
from jax import lax
from jax.experimental import pallas as pl
from jax.experimental.pallas import tpu as pltpu
from jax.sharding import PartitionSpec as P

META_ROWS = 8
STATS = 4
CODE_MAX = 32767.0
LEVELS = 16.0
SMALLEST = 1e-36
FRACTION = 2.0**30
VMEM_BYTES = 8 * 1024 * 1024


def dot(a, b, contract):
    return lax.dot_general(a, b, (contract, ((), ())), preferred_element_type=jnp.float32)


def pack_kernel(shards, capacity, kept_dev, requests, plan, *refs):
    message_refs = refs[3 : 3 + len(plan)]
    evicted_ref, weight_ref, target_ref, sems = refs[3 + len(plan) :]
    loads = [
        pltpu.make_async_copy(refs[i], refs[3 + len(plan) + i], sems.at[i]) for i in (2, 1, 0)
    ]
    for load in loads:
        load.start()
    pairs, evict_dev, width = evicted_ref.shape
    heads = pairs // requests
    slots = shards * capacity
    me = lax.axis_index("seq")
    loads[0].wait()
    loads[1].wait()
    targets = target_ref[...]
    holder = jnp.zeros_like(targets)
    for block in range(1, shards):
        holder += (targets >= block * kept_dev).astype(jnp.int32)
    centred = targets - holder * kept_dev - kept_dev // 2
    distance = jnp.where(holder >= me, holder - me, holder - me + shards)
    owned = jnp.concatenate(
        [(distance == k).astype(jnp.float32) for k in range(shards)], axis=0
    )
    before = lax.broadcasted_iota(jnp.int32, (evict_dev, evict_dev), 0) < lax.broadcasted_iota(
        jnp.int32, (evict_dev, evict_dev), 1
    )
    prefix = dot(owned.astype(jnp.bfloat16), before.astype(jnp.bfloat16), ((1,), (0,)))
    ranked = owned * prefix
    rank = ranked[0:pairs]
    for k in range(1, shards):
        rank += ranked[k * pairs : (k + 1) * pairs]
    slot = distance * capacity + rank.astype(jnp.int32)
    facts = jnp.concatenate(
        [weight_ref[...].astype(jnp.float32), centred.astype(jnp.float32)], axis=0
    ).astype(jnp.bfloat16)
    slot_index = lax.broadcasted_iota(jnp.int32, (slots, evict_dev), 0)
    meta_index = lax.broadcasted_iota(jnp.int32, (META_ROWS, slots), 0)
    loads[2].wait()
    rows, metas = [], []
    for r in range(requests):
        weights = jnp.zeros((META_ROWS, slots), jnp.float32)
        positions = jnp.zeros((META_ROWS, slots), jnp.float32)
        for h in range(heads):
            p = r * heads + h
            placing = (slot_index == slot[p : p + 1, :]).astype(jnp.float32).astype(jnp.bfloat16)
            rows.append(dot(placing, evicted_ref[p], ((1,), (0,))))
            placed = dot(facts, placing, ((1,), (1,)))
            weights = jnp.where(meta_index == h, placed[p : p + 1], weights)
            positions = jnp.where(meta_index == h, placed[pairs + p : pairs + p + 1], positions)
        metas.append(jnp.concatenate([weights, positions], axis=1))
    for message_ref, (k, members) in zip(message_refs, plan):
        message = [
            rows[r * heads + h][k * capacity : (k + 1) * capacity]
            for r in members
            for h in range(heads)
        ]
        message += [metas[r] for r in members]
        message_ref[...] = jnp.concatenate(message, axis=0).astype(jnp.bfloat16)


def load_kernel(from_ref, *refs):
    to_refs, sems = refs[:-1], refs[-1]
    each = to_refs[0].shape[0]
    copies = [
        pltpu.make_async_copy(from_ref.at[pl.ds(r * each, each)], to_ref, sems.at[r])
        for r, to_ref in enumerate(to_refs)
    ]
    for copy in copies:
        copy.start()
    for copy in copies:
        copy.wait()


def store_kernel(*refs):
    from_refs, to_ref, sems = refs[:-2], refs[-2], refs[-1]
    each = from_refs[0].shape[0]
    copies = [
        pltpu.make_async_copy(from_ref, to_ref.at[pl.ds(r * each, each)], sems.at[r])
        for r, from_ref in enumerate(from_refs)
    ]
    for copy in copies:
        copy.start()
    for copy in copies:
        copy.wait()


def merge_kernel(shards, capacity, request, places, *refs):
    cache_ref, query_ref, count_ref = refs[:3]
    message_refs = refs[3 : 3 + shards]
    before_refs, merged_ref, partial_ref = refs[3 + shards : -2], refs[-2], refs[-1]
    heads, kept_dev, width = merged_ref.shape
    head_dim = width // 2
    rows_each = query_ref.shape[1]
    slots = shards * capacity
    scale = 1.0 / math.sqrt(head_dim)
    lane = lax.broadcasted_iota(jnp.int32, (META_ROWS, slots), 1)
    weights = jnp.zeros((META_ROWS, slots), jnp.float32)
    positions = jnp.zeros((META_ROWS, slots), jnp.float32)
    received = []
    for k in range(shards):
        members, place = places[k]
        first = members * heads * capacity
        meta = message_refs[k][first : first + members * META_ROWS, :].astype(jnp.float32)
        meta = meta[place * META_ROWS : (place + 1) * META_ROWS]
        mine = jnp.logical_and(lane >= k * capacity, lane < (k + 1) * capacity)
        weights = jnp.where(mine, meta[:, 0:slots], weights)
        positions = jnp.where(mine, meta[:, slots : 2 * slots], positions)
        if capacity % 16:
            received.append(message_refs[k][...].astype(jnp.float32))
    positions = (positions + float(kept_dev // 2)).astype(jnp.int32)
    kept_index = lax.broadcasted_iota(jnp.int32, (kept_dev, slots), 0)
    ones = jnp.ones((slots, head_dim), jnp.bfloat16)
    for h in range(heads):
        if capacity % 16:
            rows = [
                m[(place * heads + h) * capacity : (place * heads + h + 1) * capacity]
                for m, (_, place) in zip(received, places)
            ]
            rows = jnp.concatenate(rows, axis=0).astype(jnp.bfloat16)
        else:
            rows = [
                m[(place * heads + h) * capacity : (place * heads + h + 1) * capacity, :]
                for m, (_, place) in zip(message_refs, places)
            ]
            rows = jnp.concatenate(rows, axis=0)
        placing = jnp.where(kept_index == positions[h : h + 1, :], weights[h : h + 1, :], 0.0)
        placing = placing.astype(jnp.bfloat16)
        summed = dot(placing, rows, ((1,), (0,)))
        share = 1.0 / (1.0 + dot(placing, ones, ((1,), (0,))))
        stored = cache_ref[h].astype(jnp.float32) + summed
        merged_ref[h, :, 0:head_dim] = (stored[:, 0:head_dim] * share).astype(jnp.bfloat16)
        merged_ref[h, :, head_dim:] = (stored[:, head_dim:] * share).astype(jnp.bfloat16)
    scores = [
        dot(query_ref[request * heads + h], merged_ref[h, :, 0:head_dim], ((1,), (1,)))
        for h in range(heads)
    ]
    scores = jnp.concatenate(scores, axis=0) * scale
    column = lax.broadcasted_iota(jnp.int32, scores.shape, 1)
    scores = jnp.where(column < count_ref[request : request + 1, :], scores, -1e30)
    top = jnp.max(scores, axis=1, keepdims=True)
    exponent = jnp.exp(scores - top)
    total = jnp.sum(exponent, axis=1, keepdims=True)
    exponent = exponent.astype(jnp.bfloat16)
    weighted = [
        dot(
            exponent[h * rows_each : (h + 1) * rows_each],
            merged_ref[h, :, head_dim:],
            ((1,), (0,)),
        )
        for h in range(heads)
    ]
    weighted = jnp.concatenate(weighted, axis=0)
    largest = jnp.max(jnp.abs(weighted), axis=1, keepdims=True)
    level = jnp.ceil(jnp.log2(jnp.maximum(largest, SMALLEST)) * LEVELS)
    codes = jnp.floor(weighted * (CODE_MAX / jnp.exp2(level / LEVELS)) + 0.5)
    codes = jnp.clip(codes, -CODE_MAX, CODE_MAX).astype(jnp.int32)
    stat_lane = lax.broadcasted_iota(jnp.int32, weighted.shape, 1)
    stats = jnp.where(stat_lane == 0, top, jnp.where(stat_lane == 1, total, level))
    stats = jnp.transpose(stats)
    top, total, level = stats[0:1], stats[1:2], stats[2:3]
    whole = jnp.floor(top)
    half = heads * rows_each // 2
    words = (codes[0:half] << 16) | (codes[half:] & 0xFFFF)
    stats = [
        whole.astype(jnp.int32),
        ((top - whole) * FRACTION).astype(jnp.int32),
        (total * (FRACTION / kept_dev)).astype(jnp.int32),
        level.astype(jnp.int32),
    ]
    for i, before_ref in enumerate(before_refs):
        partial_ref[i * half : (i + 1) * half, :] = before_ref[0:half, :]
    stats = [before_ref[half : half + STATS, :] for before_ref in before_refs] + stats
    filler = -STATS * (len(before_refs) + 1) % 8
    if filler:
        stats.append(jnp.zeros((filler, top.shape[1]), jnp.int32))
    first = len(before_refs) * half
    partial_ref[first : first + half, :] = words
    partial_ref[first + half :, :] = jnp.concatenate(stats, axis=0)


def combine_kernel(shards, heads, kept_dev, *refs):
    partial_refs = refs[:shards]
    fresh_top_ref, fresh_total_ref, fresh_ref, out_ref, ordered = refs[shards:]
    steps, requests, query_local, head_dim = out_ref.shape
    group = query_local // heads
    rows_each = steps * group
    rows_request = heads * rows_each
    half = rows_request // 2
    me = lax.axis_index("seq")
    for k in range(shards):
        source = jnp.where(me >= k, me - k, me - k + shards)
        ordered[source] = partial_refs[k][...]
    for r in range(requests):
        tops, totals, units = [fresh_top_ref[r : r + 1, :]], [fresh_total_ref[r : r + 1, :]], [1.0]
        for b in range(shards):
            stats = ordered[b, requests * half : requests * (half + STATS), :].astype(jnp.float32)
            stats = stats[r * STATS : (r + 1) * STATS]
            tops.append(stats[0:1] + stats[1:2] * (1.0 / FRACTION))
            totals.append(stats[2:3] * (kept_dev / FRACTION))
            units.append(jnp.exp2(stats[3:4] / LEVELS) * (1.0 / CODE_MAX))
        highest = functools.reduce(jnp.maximum, tops)
        scales = [jnp.exp(top - highest) for top in tops]
        total = sum(a * b for a, b in zip(totals, scales))
        factors = jnp.concatenate([s * u / total for s, u in zip(scales, units)], axis=0)
        padding = -(shards + 1) % 8
        if padding:
            factors = jnp.concatenate(
                [factors, jnp.zeros((padding, rows_request), jnp.float32)], axis=0
            )
        factors = jnp.transpose(factors)
        first = r * rows_request
        result = fresh_ref[first : first + rows_request, :] * factors[:, 0:1]
        for b in range(shards):
            words = ordered[b, r * half : (r + 1) * half, :]
            codes = jnp.concatenate([words >> 16, (words << 16) >> 16], axis=0)
            result += codes.astype(jnp.float32) * factors[:, b + 1 : b + 2]
        for s in range(steps):
            pieces = [
                result[h * rows_each + s * group : h * rows_each + (s + 1) * group]
                for h in range(heads)
            ]
            out_ref[s, r] = jnp.concatenate(pieces, axis=0).astype(jnp.bfloat16)


def fresh_block(query_rows, fresh_rows, group):
    head_dim = query_rows.shape[-1]
    scores = jnp.einsum(
        "pqd,pjd->pqj", query_rows, fresh_rows[..., :head_dim], preferred_element_type=jnp.float32
    ) * (1.0 / math.sqrt(head_dim))
    step_index = jnp.arange(query_rows.shape[1], dtype=jnp.int32) // group
    allowed = jnp.arange(fresh_rows.shape[1], dtype=jnp.int32)[None, :] <= step_index[:, None]
    scores = jnp.where(allowed[None], scores, -1e30)
    top = jnp.max(scores, axis=-1)
    exponent = jnp.exp(scores - top[..., None])
    weighted = jnp.einsum(
        "pqj,pjd->pqd",
        exponent.astype(jnp.bfloat16),
        fresh_rows[..., head_dim:],
        preferred_element_type=jnp.float32,
    )
    return (top, jnp.sum(exponent, axis=-1), weighted)


def body(cache, evicted, merge_weight, targets, kept_counts, queries, new_rows):
    req_local, head_local, kept_dev, width = cache.shape
    head_dim = width // 2
    shards = lax.axis_size("seq")
    evict_dev = evicted.shape[2]
    capacity = max(2, 2 * evict_dev // shards)
    pairs = req_local * head_local
    steps, _, query_local, _ = queries.shape
    group = query_local // head_local
    rows_each = steps * group
    vmem = pl.BlockSpec(memory_space=pltpu.VMEM)
    anywhere = pl.BlockSpec(memory_space=pl.ANY)

    def in_hbm(array):
        return pltpu.with_memory_space_constraint(array, pltpu.HBM)

    params = pltpu.CompilerParams(vmem_limit_bytes=VMEM_BYTES)

    rows_request = head_local * rows_each
    every = tuple(range(req_local))
    plan = [(k, every) for k in range(min(2, shards))]
    plan += [(k, (r,)) for r in every for k in range(2, shards)]
    packed = pl.pallas_call(
        functools.partial(pack_kernel, shards, capacity, kept_dev, req_local, plan),
        out_shape=[
            jax.ShapeDtypeStruct(
                (len(m) * (head_local * capacity + META_ROWS), width), jnp.bfloat16
            )
            for _, m in plan
        ],
        in_specs=[anywhere] * 3,
        out_specs=[vmem] * len(plan),
        scratch_shapes=[
            pltpu.VMEM((pairs, evict_dev, width), jnp.bfloat16),
            pltpu.VMEM((pairs, evict_dev), jnp.bfloat16),
            pltpu.VMEM((pairs, evict_dev), jnp.int32),
            pltpu.SemaphoreType.DMA((3,)),
        ],
        compiler_params=params,
        name="pack",
    )(
        in_hbm(evicted.reshape(pairs, evict_dev, width)),
        in_hbm(merge_weight.reshape(pairs, evict_dev)),
        in_hbm(targets.reshape(pairs, evict_dev)),
    )

    def shifted(array, k):
        return lax.ppermute(array, "seq", [(i, (i + k) % shards) for i in range(shards)])

    messages = [shifted(m, k) if k else m for m, (k, _) in zip(packed, plan)]

    query_rows = queries.reshape(steps, req_local, head_local, group, head_dim)
    query_rows = query_rows.transpose(1, 2, 0, 3, 4).reshape(pairs, rows_each, head_dim)
    fresh_rows = new_rows.transpose(1, 2, 0, 3).reshape(pairs, steps, width)
    fresh_top, fresh_total, fresh = fresh_block(query_rows, fresh_rows, group)
    fresh_top = fresh_top.reshape(req_local, rows_request)
    fresh_total = fresh_total.reshape(req_local, rows_request)
    fresh = fresh.reshape(pairs * rows_each, head_dim)

    block = jax.ShapeDtypeStruct((head_local, kept_dev, width), jnp.bfloat16)
    staged = pl.pallas_call(
        load_kernel,
        out_shape=[block] * req_local,
        in_specs=[anywhere],
        out_specs=[vmem] * req_local,
        scratch_shapes=[pltpu.SemaphoreType.DMA((req_local,))],
        compiler_params=params,
        name="stage",
    )(in_hbm(cache.reshape(pairs, kept_dev, width)))

    merged, partials = [], []
    for r in range(req_local):
        last = r == req_local - 1
        mine = [i for i, (_, m) in enumerate(plan) if r in m]
        places = [(len(plan[i][1]), plan[i][1].index(r)) for i in mine]
        parts = req_local if last else 1
        stat_rows = STATS * parts + -STATS * parts % 8
        merged_block, partial = pl.pallas_call(
            functools.partial(merge_kernel, shards, capacity, r, places),
            out_shape=[
                block,
                jax.ShapeDtypeStruct((parts * rows_request // 2 + stat_rows, head_dim), jnp.int32),
            ],
            in_specs=[vmem] * (3 + shards + parts - 1),
            out_specs=[vmem, vmem],
            input_output_aliases={0: 0},
            compiler_params=params,
            name="merge",
        )(staged[r], query_rows, kept_counts, *[messages[i] for i in mine], *partials[: parts - 1])
        merged.append(merged_block)
        partials.append(partial)
    partial = partials[-1]
    partials = [partial] + [shifted(partial, k) for k in range(shards - 1, 0, -1)][::-1]

    merged = pl.pallas_call(
        store_kernel,
        out_shape=pltpu.HBM((pairs, kept_dev, width), jnp.bfloat16),
        in_specs=[vmem] * req_local,
        out_specs=anywhere,
        scratch_shapes=[pltpu.SemaphoreType.DMA((req_local,))],
        compiler_params=params,
        name="unstage",
    )(*merged)

    attended = pl.pallas_call(
        functools.partial(combine_kernel, shards, head_local, kept_dev),
        out_shape=jax.ShapeDtypeStruct(queries.shape, jnp.bfloat16),
        in_specs=[vmem] * (shards + 3),
        out_specs=vmem,
        scratch_shapes=[pltpu.VMEM((shards,) + partial.shape, jnp.int32)],
        compiler_params=params,
        name="combine",
    )(*partials, fresh_top, fresh_total, fresh)
    return (merged.reshape(cache.shape), attended)


def solution(mesh):
    return jax.shard_map(
        body,
        mesh=mesh,
        in_specs=(
            P(("grp", "req"), "hd", "seq", None),
            P(("grp", "req"), "hd", "seq", None),
            P(("grp", "req"), "hd", "seq"),
            P(("grp", "req"), "hd", "seq"),
            P(("grp", "req"), "seq"),
            P(None, ("grp", "req"), "hd", None),
            P(None, ("grp", "req"), "hd", None),
        ),
        out_specs=(P(("grp", "req"), "hd", "seq", None), P(None, ("grp", "req"), "hd", None)),
        check_vma=False,
    )
```

```python
import functools
import math

import jax
import jax.numpy as jnp
from jax import lax
from jax.experimental import pallas as pl
from jax.experimental.pallas import tpu as pltpu
from jax.sharding import PartitionSpec as P

STATS = 4
CODE_MAX = 32767.0
LEVELS = 16.0
SMALLEST = 1e-36
FRACTION = 2.0**30
VMEM_BYTES = 8 * 1024 * 1024


def dot(a, b, contract):
    return lax.dot_general(a, b, (contract, ((), ())), preferred_element_type=jnp.float32)


def apart(holder, me, shards):
    if shards & (shards - 1):
        return jnp.where(holder >= me, holder - me, holder - me + shards)
    return jnp.bitwise_xor(holder, me)


def at_distance(i, k, shards):
    return (i + k) % shards if shards & (shards - 1) else i ^ k


def pack_kernel(shards, capacity, kept_dev, requests, plan, *refs):
    message_refs = refs[3 : 3 + len(plan)]
    evicted_ref, weight_ref, target_ref, sems = refs[3 + len(plan) :]
    loads = [
        pltpu.make_async_copy(refs[i], refs[3 + len(plan) + i], sems.at[i]) for i in (2, 1, 0)
    ]
    for load in loads:
        load.start()
    pairs, evict_dev, width = evicted_ref.shape
    slots = shards * capacity
    me = lax.axis_index("seq")
    loads[0].wait()
    loads[1].wait()
    targets = target_ref[...]
    holder = jnp.zeros_like(targets)
    for block in range(1, shards):
        holder += (targets >= block * kept_dev).astype(jnp.int32)
    centred = targets - holder * kept_dev - kept_dev // 2
    distance = apart(holder, me, shards)
    owned = jnp.concatenate(
        [(distance == k).astype(jnp.float32) for k in range(shards)], axis=0
    )
    before = lax.broadcasted_iota(jnp.int32, (evict_dev, evict_dev), 0) < lax.broadcasted_iota(
        jnp.int32, (evict_dev, evict_dev), 1
    )
    prefix = dot(owned.astype(jnp.bfloat16), before.astype(jnp.bfloat16), ((1,), (0,)))
    ranked = owned * prefix
    rank = ranked[0:pairs]
    for k in range(1, shards):
        rank += ranked[k * pairs : (k + 1) * pairs]
    slot = distance * capacity + rank.astype(jnp.int32)
    facts = jnp.concatenate(
        [weight_ref[...].astype(jnp.float32), centred.astype(jnp.float32)], axis=0
    ).astype(jnp.bfloat16)
    slot_index = lax.broadcasted_iota(jnp.int32, (slots, evict_dev), 0)
    pair_index = lax.broadcasted_iota(jnp.int32, (pairs, slots), 0)
    weights = jnp.zeros((pairs, slots), jnp.float32)
    positions = jnp.zeros((pairs, slots), jnp.float32)
    rows = []
    loads[2].wait()
    for p in range(pairs):
        placing = (slot_index == slot[p : p + 1, :]).astype(jnp.float32).astype(jnp.bfloat16)
        rows.append(dot(placing, evicted_ref[p], ((1,), (0,))))
        placed = dot(facts, placing, ((1,), (1,)))
        weights = jnp.where(pair_index == p, placed[0:pairs], weights)
        positions = jnp.where(pair_index == p, placed[pairs:], positions)
    meta = jnp.concatenate([weights, positions], axis=1)
    heads = pairs // requests
    for message_ref, (k, members) in zip(message_refs, plan):
        message = [
            rows[r * heads + h][k * capacity : (k + 1) * capacity]
            for r in members
            for h in range(heads)
        ]
        message_ref[...] = jnp.concatenate(message + [meta], axis=0).astype(jnp.bfloat16)


def load_kernel(from_ref, *refs):
    to_refs, sems = refs[:-1], refs[-1]
    each = to_refs[0].shape[0]
    copies = [
        pltpu.make_async_copy(from_ref.at[pl.ds(r * each, each)], to_ref, sems.at[r])
        for r, to_ref in enumerate(to_refs)
    ]
    for copy in copies:
        copy.start()
    for copy in copies:
        copy.wait()


def store_kernel(*refs):
    from_refs, to_ref, sems = refs[:-2], refs[-2], refs[-1]
    each = from_refs[0].shape[0]
    copies = [
        pltpu.make_async_copy(from_ref, to_ref.at[pl.ds(r * each, each)], sems.at[r])
        for r, from_ref in enumerate(from_refs)
    ]
    for copy in copies:
        copy.start()
    for copy in copies:
        copy.wait()


def merge_kernel(shards, capacity, requests, request, parts, *refs):
    cache_ref, query_ref, count_ref = refs[:3]
    message_refs = refs[3 : 3 + shards]
    before_refs = refs[3 + shards : 3 + shards + 2 * request]
    merged_ref, *out_refs = refs[3 + shards + 2 * request :]
    heads, kept_dev, width = merged_ref.shape
    pairs = requests * heads
    head_dim = width // 2
    rows_each = query_ref.shape[1]
    rows_request = heads * rows_each
    slots = shards * capacity
    scale = 1.0 / math.sqrt(head_dim)
    order = sorted(range(shards), key=lambda i: parts[i][0])
    firsts = [members.index(request) * heads * capacity for _, members in parts]
    lane = lax.broadcasted_iota(jnp.int32, (pairs, slots), 1)
    weights = jnp.zeros((pairs, slots), jnp.float32)
    positions = jnp.zeros((pairs, slots), jnp.float32)
    received = []
    for (k, members), message_ref in zip(parts, message_refs):
        meta = message_ref[len(members) * heads * capacity :, :].astype(jnp.float32)
        mine = jnp.logical_and(lane >= k * capacity, lane < (k + 1) * capacity)
        weights = jnp.where(mine, meta[:, 0:slots], weights)
        positions = jnp.where(mine, meta[:, slots : 2 * slots], positions)
        if capacity % 16:
            received.append(message_ref[...].astype(jnp.float32))
    positions, weights = positions.astype(jnp.bfloat16), weights.astype(jnp.bfloat16)
    kept_index = lax.broadcasted_iota(jnp.int32, (kept_dev, slots), 0) - kept_dev // 2
    kept_index = kept_index.astype(jnp.float32).astype(jnp.bfloat16)
    nothing = jnp.zeros((), jnp.bfloat16)
    together = 2 - heads % 2
    twin_row = lax.broadcasted_iota(jnp.int32, (together * slots, together * head_dim), 0) // slots
    twin_lane = lax.broadcasted_iota(jnp.int32, twin_row.shape, 1) // head_dim
    twin = (twin_row == twin_lane).astype(jnp.float32).astype(jnp.bfloat16)
    for first in range(0, heads, together):
        placings = []
        for h in range(first, first + together):
            p = request * heads + h
            placings.append(
                jnp.where(kept_index == positions[p : p + 1, :], weights[p : p + 1, :], nothing)
            )
        share = 1.0 / (1.0 + dot(jnp.concatenate(placings, axis=1), twin, ((1,), (0,))))
        for i, h in enumerate(range(first, first + together)):
            if capacity % 16:
                rows = [received[j][firsts[j] + h * capacity :][:capacity] for j in order]
                rows = jnp.concatenate(rows, axis=0).astype(jnp.bfloat16)
            else:
                rows = [
                    message_refs[j][pl.ds(firsts[j] + h * capacity, capacity), :] for j in order
                ]
                rows = jnp.concatenate(rows, axis=0)
            stored = cache_ref[h].astype(jnp.float32) + dot(placings[i], rows, ((1,), (0,)))
            own = share[:, i * head_dim : (i + 1) * head_dim]
            merged_ref[h, :, 0:head_dim] = (stored[:, 0:head_dim] * own).astype(jnp.bfloat16)
            merged_ref[h, :, head_dim:] = (stored[:, head_dim:] * own).astype(jnp.bfloat16)
    scores = [
        dot(query_ref[request * heads + h], merged_ref[h, :, 0:head_dim], ((1,), (1,)))
        for h in range(heads)
    ]
    scores = jnp.concatenate(scores, axis=0) * scale
    column = lax.broadcasted_iota(jnp.int32, scores.shape, 1)
    scores = jnp.where(column < count_ref[request : request + 1, :], scores, -1e30)
    top = jnp.max(scores, axis=1, keepdims=True)
    exponent = jnp.exp(scores - top)
    total = jnp.sum(exponent, axis=1, keepdims=True)
    exponent = exponent.astype(jnp.bfloat16)
    weighted = [
        dot(
            exponent[h * rows_each : (h + 1) * rows_each],
            merged_ref[h, :, head_dim:],
            ((1,), (0,)),
        )
        for h in range(heads)
    ]
    weighted = jnp.concatenate(weighted, axis=0)
    largest = jnp.max(jnp.abs(weighted), axis=1, keepdims=True)
    level = jnp.ceil(jnp.log2(jnp.maximum(largest, SMALLEST)) * LEVELS)
    codes = jnp.floor(weighted * (CODE_MAX / jnp.exp2(level / LEVELS)) + 0.5)
    codes = jnp.clip(codes, -CODE_MAX, CODE_MAX).astype(jnp.int32)
    stat_lane = lax.broadcasted_iota(jnp.int32, weighted.shape, 1)
    stats = jnp.zeros(weighted.shape, jnp.float32)
    for i, stat in enumerate((top, total, level)):
        stats = jnp.where(stat_lane == i * requests + request, stat, stats)
    if request < requests - 1:
        out_refs[0][...] = codes
        out_refs[1][...] = stats
        return
    (partial_ref,) = out_refs
    codes = [before_refs[2 * r][...] for r in range(request)] + [codes]
    codes = jnp.concatenate(codes, axis=0)
    for r in range(request):
        stats += before_refs[2 * r + 1][...]
    half = requests * rows_request // 2
    partial_ref[0:half, :] = (codes[0:half] << 16) | (codes[half:] & 0xFFFF)
    stats = jnp.transpose(stats)
    top, total, level = (stats[i * requests : (i + 1) * requests] for i in range(3))
    whole = jnp.floor(top)
    stats = [
        whole.astype(jnp.int32),
        ((top - whole) * FRACTION).astype(jnp.int32),
        (total * (FRACTION / kept_dev)).astype(jnp.int32),
        level.astype(jnp.int32),
    ]
    filler = -STATS * requests % 8
    if filler:
        stats.append(jnp.zeros((filler, rows_request), jnp.int32))
    partial_ref[half:, :] = jnp.concatenate(stats, axis=0)


def combine_kernel(shards, heads, kept_dev, distances, *refs):
    partial_refs = refs[:shards]
    fresh_top_ref, fresh_total_ref, fresh_ref, out_ref, ordered = refs[shards:]
    steps, requests, query_local, head_dim = out_ref.shape
    group = query_local // heads
    rows_each = steps * group
    rows_request = heads * rows_each
    half = requests * rows_request // 2
    me = lax.axis_index("seq")
    for k, partial_ref in zip(distances, partial_refs):
        source = jnp.where(me >= k, me - k, me - k + shards)
        ordered[source] = partial_ref[...]
    tops, totals, units = [fresh_top_ref[...]], [fresh_total_ref[...]], [1.0]
    for b in range(shards):
        stats = ordered[b, half : half + STATS * requests, :].astype(jnp.float32)
        whole, rest, total, level = (
            stats[i * requests : (i + 1) * requests] for i in range(STATS)
        )
        tops.append(whole + rest * (1.0 / FRACTION))
        totals.append(total * (kept_dev / FRACTION))
        units.append(jnp.exp2(level / LEVELS) * (1.0 / CODE_MAX))
    highest = functools.reduce(jnp.maximum, tops)
    scales = [jnp.exp(top - highest) for top in tops]
    share = 1.0 / sum(a * b for a, b in zip(totals, scales))
    factors = [s * u * share for s, u in zip(scales, units)]
    padding = -len(factors) * requests % 8
    if padding:
        factors.append(jnp.zeros((padding, rows_request), jnp.float32))
    factors = jnp.transpose(jnp.concatenate(factors, axis=0))
    for r in range(requests):
        first = r * rows_request
        result = fresh_ref[first : first + rows_request, :] * factors[:, r : r + 1]
        low = first % half
        for b in range(shards):
            words = ordered[b, low : low + rows_request, :]
            codes = words >> 16 if first < half else (words << 16) >> 16
            column = (b + 1) * requests + r
            result += codes.astype(jnp.float32) * factors[:, column : column + 1]
        for s in range(steps):
            pieces = [
                result[h * rows_each + s * group : h * rows_each + (s + 1) * group]
                for h in range(heads)
            ]
            out_ref[s, r] = jnp.concatenate(pieces, axis=0).astype(jnp.bfloat16)


def fresh_block(query_rows, fresh_rows, group):
    head_dim = query_rows.shape[-1]
    scores = jnp.einsum(
        "pqd,pjd->pqj", query_rows, fresh_rows[..., :head_dim], preferred_element_type=jnp.float32
    ) * (1.0 / math.sqrt(head_dim))
    step_index = jnp.arange(query_rows.shape[1], dtype=jnp.int32) // group
    allowed = jnp.arange(fresh_rows.shape[1], dtype=jnp.int32)[None, :] <= step_index[:, None]
    scores = jnp.where(allowed[None], scores, -1e30)
    top = jnp.max(scores, axis=-1)
    exponent = jnp.exp(scores - top[..., None])
    weighted = jnp.einsum(
        "pqj,pjd->pqd",
        exponent.astype(jnp.bfloat16),
        fresh_rows[..., head_dim:],
        preferred_element_type=jnp.float32,
    )
    return (top, jnp.sum(exponent, axis=-1), weighted)


def body(cache, evicted, merge_weight, targets, kept_counts, queries, new_rows):
    req_local, head_local, kept_dev, width = cache.shape
    head_dim = width // 2
    shards = lax.axis_size("seq")
    evict_dev = evicted.shape[2]
    capacity = max(2, 2 * evict_dev // shards)
    pairs = req_local * head_local
    steps, _, query_local, _ = queries.shape
    group = query_local // head_local
    rows_each = steps * group
    vmem = pl.BlockSpec(memory_space=pltpu.VMEM)
    anywhere = pl.BlockSpec(memory_space=pl.ANY)

    def in_hbm(array):
        return pltpu.with_memory_space_constraint(array, pltpu.HBM)

    params = pltpu.CompilerParams(vmem_limit_bytes=VMEM_BYTES)

    rows_request = head_local * rows_each
    distances = [0] + sorted(range(1, shards), key=lambda k: (k & (k - 1), -k))
    every = tuple(range(req_local))
    plan = [(k, every) for k in distances[:-1]] + [(distances[-1], (r,)) for r in every]
    packed = pl.pallas_call(
        functools.partial(pack_kernel, shards, capacity, kept_dev, req_local, plan),
        out_shape=[
            jax.ShapeDtypeStruct((len(m) * head_local * capacity + pairs, width), jnp.bfloat16)
            for _, m in plan
        ],
        in_specs=[anywhere] * 3,
        out_specs=[vmem] * len(plan),
        scratch_shapes=[
            pltpu.VMEM((pairs, evict_dev, width), jnp.bfloat16),
            pltpu.VMEM((pairs, evict_dev), jnp.bfloat16),
            pltpu.VMEM((pairs, evict_dev), jnp.int32),
            pltpu.SemaphoreType.DMA((3,)),
        ],
        compiler_params=params,
        name="pack",
    )(
        in_hbm(evicted.reshape(pairs, evict_dev, width)),
        in_hbm(merge_weight.reshape(pairs, evict_dev)),
        in_hbm(targets.reshape(pairs, evict_dev)),
    )

    messages = [packed[0]]
    for (k, _), message in zip(plan[1:], packed[1:]):
        pairing = [(i, at_distance(i, k, shards)) for i in range(shards)]
        messages.append(lax.ppermute(message, "seq", pairing))

    query_rows = queries.reshape(steps, req_local, head_local, group, head_dim)
    query_rows = query_rows.transpose(1, 2, 0, 3, 4).reshape(pairs, rows_each, head_dim)
    fresh_rows = new_rows.transpose(1, 2, 0, 3).reshape(pairs, steps, width)
    fresh_top, fresh_total, fresh = fresh_block(query_rows, fresh_rows, group)
    fresh_top = fresh_top.reshape(req_local, rows_request)
    fresh_total = fresh_total.reshape(req_local, rows_request)
    fresh = fresh.reshape(pairs * rows_each, head_dim)

    block = jax.ShapeDtypeStruct((head_local, kept_dev, width), jnp.bfloat16)
    staged = pl.pallas_call(
        load_kernel,
        out_shape=[block] * req_local,
        in_specs=[anywhere],
        out_specs=[vmem] * req_local,
        scratch_shapes=[pltpu.SemaphoreType.DMA((req_local,))],
        compiler_params=params,
        name="stage",
    )(in_hbm(cache.reshape(pairs, kept_dev, width)))

    stat_rows = STATS * req_local + -STATS * req_local % 8
    partial_shape = (pairs * rows_each // 2 + stat_rows, head_dim)
    kinds = [((rows_request, head_dim), jnp.int32), ((rows_request, head_dim), jnp.float32)]
    merged, before = [], []
    for r in range(req_local):
        mine = [i for i, (_, m) in enumerate(plan) if r in m]
        if r == req_local - 1:
            kinds = [(partial_shape, jnp.int32)]
        merged_block, *out = pl.pallas_call(
            functools.partial(
                merge_kernel, shards, capacity, req_local, r, [plan[i] for i in mine]
            ),
            out_shape=[block] + [jax.ShapeDtypeStruct(*kind) for kind in kinds],
            in_specs=[vmem] * (3 + shards + len(before)),
            out_specs=[vmem] * (1 + len(kinds)),
            input_output_aliases={0: 0},
            compiler_params=params,
            name="merge",
        )(staged[r], query_rows, kept_counts, *[messages[i] for i in mine], *before)
        merged.append(merged_block)
        before += out
    partial = before[-1]

    shifts = list(range(shards))
    partials = [partial]
    for k in shifts[1:]:
        pairing = [(i, (i + k) % shards) for i in range(shards)]
        partials.append(lax.ppermute(partial, "seq", pairing))

    merged = pl.pallas_call(
        store_kernel,
        out_shape=pltpu.HBM((pairs, kept_dev, width), jnp.bfloat16),
        in_specs=[vmem] * req_local,
        out_specs=anywhere,
        scratch_shapes=[pltpu.SemaphoreType.DMA((req_local,))],
        compiler_params=params,
        name="unstage",
    )(*merged)

    attended = pl.pallas_call(
        functools.partial(combine_kernel, shards, head_local, kept_dev, shifts),
        out_shape=jax.ShapeDtypeStruct(queries.shape, jnp.bfloat16),
        in_specs=[vmem] * (shards + 3),
        out_specs=vmem,
        scratch_shapes=[pltpu.VMEM((shards,) + partial.shape, jnp.int32)],
        compiler_params=params,
        name="combine",
    )(*partials, fresh_top, fresh_total, fresh)
    return (merged.reshape(cache.shape), attended)


def solution(mesh):
    return jax.shard_map(
        body,
        mesh=mesh,
        in_specs=(
            P(("grp", "req"), "hd", "seq", None),
            P(("grp", "req"), "hd", "seq", None),
            P(("grp", "req"), "hd", "seq"),
            P(("grp", "req"), "hd", "seq"),
            P(("grp", "req"), "seq"),
            P(None, ("grp", "req"), "hd", None),
            P(None, ("grp", "req"), "hd", None),
        ),
        out_specs=(P(("grp", "req"), "hd", "seq", None), P(None, ("grp", "req"), "hd", None)),
        check_vma=False,
    )
```

```python
import functools
import math

import jax
import jax.numpy as jnp
from jax import lax
from jax.experimental import pallas as pl
from jax.experimental.pallas import tpu as pltpu
from jax.sharding import PartitionSpec as P

STATS = 4
CODE_MAX = 32767.0
LEVELS = 16.0
SMALLEST = 1e-36
FRACTION = 2.0**30
VMEM_BYTES = 8 * 1024 * 1024


def dot(a, b, contract):
    return lax.dot_general(a, b, (contract, ((), ())), preferred_element_type=jnp.float32)


def apart(holder, me, shards):
    if shards & (shards - 1):
        return jnp.where(holder >= me, holder - me, holder - me + shards)
    return jnp.bitwise_xor(holder, me)


def at_distance(i, k, shards):
    return (i + k) % shards if shards & (shards - 1) else i ^ k


def pack_kernel(shards, capacity, kept_dev, requests, plan, *refs):
    message_refs = refs[3 : 3 + len(plan)]
    evicted_ref, weight_ref, target_ref, sems = refs[3 + len(plan) :]
    loads = [
        pltpu.make_async_copy(refs[i], refs[3 + len(plan) + i], sems.at[i]) for i in (2, 1, 0)
    ]
    for load in loads:
        load.start()
    pairs, evict_dev, width = evicted_ref.shape
    slots = shards * capacity
    me = lax.axis_index("seq")
    loads[0].wait()
    loads[1].wait()
    targets = target_ref[...]
    holder = jnp.zeros_like(targets)
    for block in range(1, shards):
        holder += (targets >= block * kept_dev).astype(jnp.int32)
    centred = targets - holder * kept_dev - kept_dev // 2
    distance = apart(holder, me, shards)
    owned = jnp.concatenate(
        [(distance == k).astype(jnp.float32) for k in range(shards)], axis=0
    )
    before = lax.broadcasted_iota(jnp.int32, (evict_dev, evict_dev), 0) < lax.broadcasted_iota(
        jnp.int32, (evict_dev, evict_dev), 1
    )
    prefix = dot(owned.astype(jnp.bfloat16), before.astype(jnp.bfloat16), ((1,), (0,)))
    ranked = owned * prefix
    rank = ranked[0:pairs]
    for k in range(1, shards):
        rank += ranked[k * pairs : (k + 1) * pairs]
    slot = distance * capacity + rank.astype(jnp.int32)
    facts = jnp.concatenate(
        [weight_ref[...].astype(jnp.float32), centred.astype(jnp.float32)], axis=0
    ).astype(jnp.bfloat16)
    slot_index = lax.broadcasted_iota(jnp.int32, (slots, evict_dev), 0)
    pair_index = lax.broadcasted_iota(jnp.int32, (pairs, slots), 0)
    weights = jnp.zeros((pairs, slots), jnp.float32)
    positions = jnp.zeros((pairs, slots), jnp.float32)
    rows = []
    loads[2].wait()
    for p in range(pairs):
        placing = (slot_index == slot[p : p + 1, :]).astype(jnp.float32).astype(jnp.bfloat16)
        rows.append(dot(placing, evicted_ref[p], ((1,), (0,))))
        placed = dot(facts, placing, ((1,), (1,)))
        weights = jnp.where(pair_index == p, placed[0:pairs], weights)
        positions = jnp.where(pair_index == p, placed[pairs:], positions)
    meta = jnp.concatenate([weights, positions], axis=1)
    heads = pairs // requests
    for message_ref, (k, members) in zip(message_refs, plan):
        message = [
            rows[r * heads + h][k * capacity : (k + 1) * capacity]
            for r in members
            for h in range(heads)
        ]
        message_ref[...] = jnp.concatenate(message + [meta], axis=0).astype(jnp.bfloat16)


def load_kernel(from_ref, *refs):
    to_refs, sems = refs[:-1], refs[-1]
    each = to_refs[0].shape[0]
    copies = [
        pltpu.make_async_copy(from_ref.at[pl.ds(r * each, each)], to_ref, sems.at[r])
        for r, to_ref in enumerate(to_refs)
    ]
    for copy in copies:
        copy.start()
    for copy in copies:
        copy.wait()


def store_kernel(*refs):
    from_refs, to_ref, sems = refs[:-2], refs[-2], refs[-1]
    each = from_refs[0].shape[0]
    copies = [
        pltpu.make_async_copy(from_ref, to_ref.at[pl.ds(r * each, each)], sems.at[r])
        for r, from_ref in enumerate(from_refs)
    ]
    for copy in copies:
        copy.start()
    for copy in copies:
        copy.wait()


def merge_kernel(shards, capacity, requests, request, parts, *refs):
    cache_ref, query_ref, count_ref = refs[:3]
    message_refs = refs[3 : 3 + shards]
    before_refs = refs[3 + shards : 3 + shards + 2 * request]
    merged_ref, *out_refs = refs[3 + shards + 2 * request :]
    heads, kept_dev, width = merged_ref.shape
    pairs = requests * heads
    head_dim = width // 2
    rows_each = query_ref.shape[1]
    rows_request = heads * rows_each
    slots = shards * capacity
    scale = 1.0 / math.sqrt(head_dim)
    order = sorted(range(shards), key=lambda i: parts[i][0])
    firsts = [members.index(request) * heads * capacity for _, members in parts]
    lane = lax.broadcasted_iota(jnp.int32, (pairs, slots), 1)
    weights = jnp.zeros((pairs, slots), jnp.float32)
    positions = jnp.zeros((pairs, slots), jnp.float32)
    received = []
    for (k, members), message_ref in zip(parts, message_refs):
        meta = message_ref[len(members) * heads * capacity :, :].astype(jnp.float32)
        mine = jnp.logical_and(lane >= k * capacity, lane < (k + 1) * capacity)
        weights = jnp.where(mine, meta[:, 0:slots], weights)
        positions = jnp.where(mine, meta[:, slots : 2 * slots], positions)
        if capacity % 16:
            received.append(message_ref[...].astype(jnp.float32))
    positions, weights = positions.astype(jnp.bfloat16), weights.astype(jnp.bfloat16)
    kept_index = lax.broadcasted_iota(jnp.int32, (kept_dev, slots), 0) - kept_dev // 2
    kept_index = kept_index.astype(jnp.float32).astype(jnp.bfloat16)
    nothing = jnp.zeros((), jnp.bfloat16)
    together = 2 - heads % 2
    twin_row = lax.broadcasted_iota(jnp.int32, (together * slots, together * head_dim), 0) // slots
    twin_lane = lax.broadcasted_iota(jnp.int32, twin_row.shape, 1) // head_dim
    twin = (twin_row == twin_lane).astype(jnp.float32).astype(jnp.bfloat16)
    for first in range(0, heads, together):
        placings = []
        for h in range(first, first + together):
            p = request * heads + h
            placings.append(
                jnp.where(kept_index == positions[p : p + 1, :], weights[p : p + 1, :], nothing)
            )
        share = 1.0 / (1.0 + dot(jnp.concatenate(placings, axis=1), twin, ((1,), (0,))))
        for i, h in enumerate(range(first, first + together)):
            if capacity % 16:
                rows = [received[j][firsts[j] + h * capacity :][:capacity] for j in order]
                rows = jnp.concatenate(rows, axis=0).astype(jnp.bfloat16)
            else:
                rows = [
                    message_refs[j][pl.ds(firsts[j] + h * capacity, capacity), :] for j in order
                ]
                rows = jnp.concatenate(rows, axis=0)
            stored = cache_ref[h].astype(jnp.float32) + dot(placings[i], rows, ((1,), (0,)))
            own = share[:, i * head_dim : (i + 1) * head_dim]
            merged_ref[h, :, 0:head_dim] = (stored[:, 0:head_dim] * own).astype(jnp.bfloat16)
            merged_ref[h, :, head_dim:] = (stored[:, head_dim:] * own).astype(jnp.bfloat16)
    scores = [
        dot(query_ref[request * heads + h], merged_ref[h, :, 0:head_dim], ((1,), (1,)))
        for h in range(heads)
    ]
    scores = jnp.concatenate(scores, axis=0) * scale
    column = lax.broadcasted_iota(jnp.int32, scores.shape, 1)
    scores = jnp.where(column < count_ref[request : request + 1, :], scores, -1e30)
    top = jnp.max(scores, axis=1, keepdims=True)
    exponent = jnp.exp(scores - top)
    total = jnp.sum(exponent, axis=1, keepdims=True)
    exponent = exponent.astype(jnp.bfloat16)
    weighted = [
        dot(
            exponent[h * rows_each : (h + 1) * rows_each],
            merged_ref[h, :, head_dim:],
            ((1,), (0,)),
        )
        for h in range(heads)
    ]
    weighted = jnp.concatenate(weighted, axis=0)
    largest = jnp.max(jnp.abs(weighted), axis=1, keepdims=True)
    level = jnp.ceil(jnp.log2(jnp.maximum(largest, SMALLEST)) * LEVELS)
    codes = jnp.floor(weighted * (CODE_MAX * jnp.exp2(level * (-1.0 / LEVELS))) + 0.5)
    codes = jnp.clip(codes, -CODE_MAX, CODE_MAX).astype(jnp.int32)
    stat_lane = lax.broadcasted_iota(jnp.int32, weighted.shape, 1)
    stats = jnp.zeros(weighted.shape, jnp.float32)
    for i, stat in enumerate((top, total, level)):
        stats = jnp.where(stat_lane == i * requests + request, stat, stats)
    if request < requests - 1:
        out_refs[0][...] = codes
        out_refs[1][...] = stats
        return
    (partial_ref,) = out_refs
    codes = [before_refs[2 * r][...] for r in range(request)] + [codes]
    codes = jnp.concatenate(codes, axis=0)
    for r in range(request):
        stats += before_refs[2 * r + 1][...]
    half = requests * rows_request // 2
    partial_ref[0:half, :] = (codes[0:half] << 16) | (codes[half:] & 0xFFFF)
    stats = jnp.transpose(stats)
    top, total, level = (stats[i * requests : (i + 1) * requests] for i in range(3))
    whole = jnp.floor(top)
    stats = [
        whole.astype(jnp.int32),
        ((top - whole) * FRACTION).astype(jnp.int32),
        (total * (FRACTION / kept_dev)).astype(jnp.int32),
        level.astype(jnp.int32),
    ]
    filler = -STATS * requests % 8
    if filler:
        stats.append(jnp.zeros((filler, rows_request), jnp.int32))
    partial_ref[half:, :] = jnp.concatenate(stats, axis=0)


def combine_kernel(shards, heads, kept_dev, distances, *refs):
    partial_refs = refs[:shards]
    fresh_top_ref, fresh_total_ref, fresh_ref, out_ref, ordered = refs[shards:]
    steps, requests, query_local, head_dim = out_ref.shape
    group = query_local // heads
    rows_each = steps * group
    rows_request = heads * rows_each
    half = requests * rows_request // 2
    me = lax.axis_index("seq")
    for k, partial_ref in zip(distances, partial_refs):
        source = jnp.where(me >= k, me - k, me - k + shards)
        ordered[source] = partial_ref[...]
    tops, totals, units = [fresh_top_ref[...]], [fresh_total_ref[...]], [1.0]
    for b in range(shards):
        stats = ordered[b, half : half + STATS * requests, :].astype(jnp.float32)
        whole, rest, total, level = (
            stats[i * requests : (i + 1) * requests] for i in range(STATS)
        )
        tops.append(whole + rest * (1.0 / FRACTION))
        totals.append(total * (kept_dev / FRACTION))
        units.append(jnp.exp2(level / LEVELS) * (1.0 / CODE_MAX))
    highest = functools.reduce(jnp.maximum, tops)
    scales = [jnp.exp(top - highest) for top in tops]
    share = 1.0 / sum(a * b for a, b in zip(totals, scales))
    factors = [s * u * share for s, u in zip(scales, units)]
    padding = -len(factors) * requests % 8
    if padding:
        factors.append(jnp.zeros((padding, rows_request), jnp.float32))
    factors = jnp.transpose(jnp.concatenate(factors, axis=0))
    for r in range(requests):
        first = r * rows_request
        result = fresh_ref[first : first + rows_request, :] * factors[:, r : r + 1]
        low = first % half
        for b in range(shards):
            words = ordered[b, low : low + rows_request, :]
            codes = words >> 16 if first < half else (words << 16) >> 16
            column = (b + 1) * requests + r
            result += codes.astype(jnp.float32) * factors[:, column : column + 1]
        for s in range(steps):
            pieces = [
                result[h * rows_each + s * group : h * rows_each + (s + 1) * group]
                for h in range(heads)
            ]
            out_ref[s, r] = jnp.concatenate(pieces, axis=0).astype(jnp.bfloat16)


def fresh_block(query_rows, fresh_rows, group):
    head_dim = query_rows.shape[-1]
    scores = jnp.einsum(
        "pqd,pjd->pqj", query_rows, fresh_rows[..., :head_dim], preferred_element_type=jnp.float32
    ) * (1.0 / math.sqrt(head_dim))
    step_index = jnp.arange(query_rows.shape[1], dtype=jnp.int32) // group
    allowed = jnp.arange(fresh_rows.shape[1], dtype=jnp.int32)[None, :] <= step_index[:, None]
    scores = jnp.where(allowed[None], scores, -1e30)
    top = jnp.max(scores, axis=-1)
    exponent = jnp.exp(scores - top[..., None])
    weighted = jnp.einsum(
        "pqj,pjd->pqd",
        exponent.astype(jnp.bfloat16),
        fresh_rows[..., head_dim:],
        preferred_element_type=jnp.float32,
    )
    return (top, jnp.sum(exponent, axis=-1), weighted)


def body(cache, evicted, merge_weight, targets, kept_counts, queries, new_rows):
    req_local, head_local, kept_dev, width = cache.shape
    head_dim = width // 2
    shards = lax.axis_size("seq")
    evict_dev = evicted.shape[2]
    capacity = max(2, 2 * evict_dev // shards)
    pairs = req_local * head_local
    steps, _, query_local, _ = queries.shape
    group = query_local // head_local
    rows_each = steps * group
    vmem = pl.BlockSpec(memory_space=pltpu.VMEM)
    anywhere = pl.BlockSpec(memory_space=pl.ANY)

    def in_hbm(array):
        return pltpu.with_memory_space_constraint(array, pltpu.HBM)

    params = pltpu.CompilerParams(vmem_limit_bytes=VMEM_BYTES)

    rows_request = head_local * rows_each
    distances = [0] + sorted(range(1, shards), key=lambda k: (k & (k - 1), -k))
    every = tuple(range(req_local))
    plan = [(k, every) for k in distances[:-1]] + [(distances[-1], (r,)) for r in every]
    def pack(plan):
        return pl.pallas_call(
            functools.partial(pack_kernel, shards, capacity, kept_dev, req_local, plan),
            out_shape=[
                jax.ShapeDtypeStruct((len(m) * head_local * capacity + pairs, width), jnp.bfloat16)
                for _, m in plan
            ],
            in_specs=[anywhere] * 3,
            out_specs=[vmem] * len(plan),
            scratch_shapes=[
                pltpu.VMEM((pairs, evict_dev, width), jnp.bfloat16),
                pltpu.VMEM((pairs, evict_dev), jnp.bfloat16),
                pltpu.VMEM((pairs, evict_dev), jnp.int32),
                pltpu.SemaphoreType.DMA((3,)),
            ],
            compiler_params=params,
            name="pack",
        )(
            in_hbm(evicted.reshape(pairs, evict_dev, width)),
            in_hbm(merge_weight.reshape(pairs, evict_dev)),
            in_hbm(targets.reshape(pairs, evict_dev)),
        )

    own, packed = pack(plan[:1]), pack(plan[1:])
    messages = list(own)
    for (k, _), message in zip(plan[1:], packed):
        pairing = [(i, at_distance(i, k, shards)) for i in range(shards)]
        messages.append(lax.ppermute(message, "seq", pairing))

    query_rows = queries.reshape(steps, req_local, head_local, group, head_dim)
    query_rows = query_rows.transpose(1, 2, 0, 3, 4).reshape(pairs, rows_each, head_dim)
    fresh_rows = new_rows.transpose(1, 2, 0, 3).reshape(pairs, steps, width)
    fresh_top, fresh_total, fresh = fresh_block(query_rows, fresh_rows, group)
    fresh_top = fresh_top.reshape(req_local, rows_request)
    fresh_total = fresh_total.reshape(req_local, rows_request)
    fresh = fresh.reshape(pairs * rows_each, head_dim)

    block = jax.ShapeDtypeStruct((head_local, kept_dev, width), jnp.bfloat16)
    staged = pl.pallas_call(
        load_kernel,
        out_shape=[block] * req_local,
        in_specs=[anywhere],
        out_specs=[vmem] * req_local,
        scratch_shapes=[pltpu.SemaphoreType.DMA((req_local,))],
        compiler_params=params,
        name="stage",
    )(in_hbm(cache.reshape(pairs, kept_dev, width)))

    stat_rows = STATS * req_local + -STATS * req_local % 8
    partial_shape = (pairs * rows_each // 2 + stat_rows, head_dim)
    kinds = [((rows_request, head_dim), jnp.int32), ((rows_request, head_dim), jnp.float32)]
    merged, before = [], []
    for r in range(req_local):
        mine = [i for i, (_, m) in enumerate(plan) if r in m]
        if r == req_local - 1:
            kinds = [(partial_shape, jnp.int32)]
        merged_block, *out = pl.pallas_call(
            functools.partial(
                merge_kernel, shards, capacity, req_local, r, [plan[i] for i in mine]
            ),
            out_shape=[block] + [jax.ShapeDtypeStruct(*kind) for kind in kinds],
            in_specs=[vmem] * (3 + shards + len(before)),
            out_specs=[vmem] * (1 + len(kinds)),
            input_output_aliases={0: 0},
            compiler_params=params,
            name="merge",
        )(staged[r], query_rows, kept_counts, *[messages[i] for i in mine], *before)
        merged.append(merged_block)
        before += out
    partial = before[-1]

    shifts = list(range(shards))
    partials = [partial]
    for k in shifts[1:]:
        pairing = [(i, (i + k) % shards) for i in range(shards)]
        partials.append(lax.ppermute(partial, "seq", pairing))

    merged = pl.pallas_call(
        store_kernel,
        out_shape=pltpu.HBM((pairs, kept_dev, width), jnp.bfloat16),
        in_specs=[vmem] * req_local,
        out_specs=anywhere,
        scratch_shapes=[pltpu.SemaphoreType.DMA((req_local,))],
        compiler_params=params,
        name="unstage",
    )(*merged)

    attended = pl.pallas_call(
        functools.partial(combine_kernel, shards, head_local, kept_dev, shifts),
        out_shape=jax.ShapeDtypeStruct(queries.shape, jnp.bfloat16),
        in_specs=[vmem] * (shards + 3),
        out_specs=vmem,
        scratch_shapes=[pltpu.VMEM((shards,) + partial.shape, jnp.int32)],
        compiler_params=params,
        name="combine",
    )(*partials, fresh_top, fresh_total, fresh)
    return (merged.reshape(cache.shape), attended)


def solution(mesh):
    return jax.shard_map(
        body,
        mesh=mesh,
        in_specs=(
            P(("grp", "req"), "hd", "seq", None),
            P(("grp", "req"), "hd", "seq", None),
            P(("grp", "req"), "hd", "seq"),
            P(("grp", "req"), "hd", "seq"),
            P(("grp", "req"), "seq"),
            P(None, ("grp", "req"), "hd", None),
            P(None, ("grp", "req"), "hd", None),
        ),
        out_specs=(P(("grp", "req"), "hd", "seq", None), P(None, ("grp", "req"), "hd", None)),
        check_vma=False,
    )
```
